512 devices in a mesh: section: 8 (over y), expert: 64 (over x, z, core).
Axes of the slice: x: 4, y: 8, z: 8, core: 2. Of those that a mesh axis runs over, the one named last changes fastest.
Arguments:
- layer_input: bfloat16 [8, 4096, 2048], P('section', 'expert'), may hold values from -6 to 6
- out_grad: bfloat16 [8, 4096, 2048], P('section', 'expert'), may hold values from -6 to 6
- norm_gain: float32 [8, 2048], P('section'), may hold values from 0.5 to 1.5
- expert_ids: int32 [8, 4096, 8], P('section', 'expert'), may hold values from 0 to 127, all different within a row; in each aligned block of 64 rows (0 to 63, 64 to 127, ..., all dimensions but the last counted through in order) at most 8 rows name the same one
- combine: bfloat16 [8, 4096, 8], P('section', 'expert'), may hold values from 0.049804688 to 0.29882812
- w_gate: bfloat16 [8, 12288, 2048], P('section', 'expert'), may hold values from -0.125 to 0.125
- w_up: bfloat16 [8, 12288, 2048], P('section', 'expert'), may hold values from -0.125 to 0.125
- w_down: bfloat16 [8, 12288, 2048], P('section', 'expert'), may hold values from -0.21875 to 0.21875
Outputs:
- passed_grad: bfloat16 [8, 4096, 2048], P('section', 'expert')
- comb_grad: bfloat16 [8, 4096, 8], P('section', 'expert')
- gain_grad: float32 [8, 2048], P('section')
The draws below stay inside these ranges and needn't reach their ends.
Inputs may be any that keep to these rules, and one draw needn't show every extreme that they name: `expert_ids`: A token names 8 different experts. Within the tokens of one device (aligned blocks of 64 tokens of a section) no expert is named by more than 8 tokens, a bound that some block reaches.
All inputs are finite; a program needn't handle non-finite values.
Results may differ from the reference program's by a relative error of at most 0.0075.
Values may be sent and summed in bfloat16 or wider, within the bound.
A program may use at most 64 MiB of HBM per device.

```python
import math
import jax
import jax.numpy as jnp
import numpy as np
from jax import lax

D = 2048
FFE = 768
TOP = 8
ALL_EXPERTS = 128
EXPERTS = 16
TOK_DEV = 64
SECTIONS = 8
SPLIT = 4
TOKENS = 4096
CAP = 8
N_EXPERT = 64


def block_levels(key, dims, cuts, least, top_value):
    loudness = 1.0
    for dim, blocks in cuts:
        steps = jax.random.uniform(jax.random.fold_in(jax.random.fold_in(key, 6), dim), (blocks,), jnp.float32, least / len(cuts), top_value / len(cuts))
        loudness = loudness * jnp.repeat(jnp.exp(steps), dims[dim] // blocks).reshape((-1,) + (1,) * (len(dims) - 1 - dim))
    return loudness


def shared_out(rng, own, number, rows, count, top, limit, lean):
    order = jax.random.permutation(rng, count)
    heavy_load, common = load_shares(count, rows * top, limit, lean, True), load_shares(count, rows * top, limit, lean, False)
    places = jnp.arange(count)

    def named(lengths, offset_by):
        used = int((lengths > 0).sum())
        fixed = max(1, used // 4)
        passed = fixed + (places - fixed + offset_by * (used - fixed)) % max(1, count - fixed)
        return jnp.zeros((count,), jnp.int32).at[order[jnp.where(places < fixed, places, passed)]].set(jnp.asarray(lengths, jnp.int32))

    lengths = jnp.where(number % 4 == 0, named(heavy_load, number // 4), named(common, number - number // 4 - 1))
    mixed = jax.random.permutation(jax.random.fold_in(own, 3), count)
    source_of, taker = mixed[0:count // 2 * 2:2], mixed[1:count // 2 * 2:2]
    slack = jnp.minimum(lengths[source_of] - 1, limit - lengths[taker]) // 2
    slack = jnp.where((source_of == order[0]) | (taker == order[0]) | (lengths[taker] == 0), 0, jnp.maximum(slack, 0))
    passed = jax.random.randint(jax.random.fold_in(own, 4), (count // 2,), 0, 1 << 20) % (slack + 1)
    lengths = lengths.at[source_of].add(-passed).at[taker].add(passed)
    members = jnp.searchsorted(jnp.cumsum(lengths), jnp.arange(rows * top), side="right").astype(jnp.int32)
    listing = members.reshape(top, rows).T
    listing = listing[jax.random.permutation(jax.random.fold_in(own, 1), rows)]
    offset_by = jax.random.randint(jax.random.fold_in(own, 2), (rows, 1), 0, top)
    return jnp.take_along_axis(listing, (jnp.arange(top)[None, :] + offset_by) % top, axis=1)


def load_shares(amount, total, limit, lean, full):
    weights = [(1 << 20) // math.isqrt(rank ** lean) + 1 for rank in range(1, amount + 1)]
    largest = limit if full else min(limit, max(-(-total // amount), total * weights[0] // sum(weights)))
    least = 1 if total - largest >= amount - 1 else 0
    counts, surplus = [largest] + [least] * (amount - 1), total - largest - least * (amount - 1)
    while surplus > 0:
        movable = [i for i in range(1, amount) if counts[i] < largest] or [i for i in range(1, amount) if counts[i] < limit]
        mass, budget = sum([weights[i] for i in movable]), surplus
        for i in movable:
            extra = min(limit - counts[i], max(1, budget * weights[i] // mass), surplus)
            counts[i] = counts[i] + extra
            surplus = surplus - extra
    return np.array(counts)


def scatter_about(rng, dims, width, reach, shards=(), held_as=jnp.bfloat16):
    array = width * jax.random.normal(rng, dims, jnp.float32)
    if shards:
        array = array * block_levels(rng, dims, shards, -0.22, 0.18)
    return jnp.clip(array, -reach, reach).astype(held_as)


def setup_inputs(seed: int = 0) -> dict:
    streams_of = jax.random.split(jax.random.key(seed), 9)
    layer_input = scatter_about(streams_of[0], (SECTIONS, TOKENS, D), 1.0, 6.0, ((0, 8), (1, 64)))
    out_grad = scatter_about(streams_of[1], (SECTIONS, TOKENS, D), 1.0, 6.0, ((0, 8), (1, 64)))
    norm_gain = jnp.clip(1.0 + 0.1 * jax.random.normal(streams_of[2], (SECTIONS, D), jnp.float32), 0.5, 1.5)
    expert_ids_keys = jax.random.split(jax.random.fold_in(streams_of[3], 1), SECTIONS * TOKENS // TOK_DEV)
    expert_ids_turns = jax.random.permutation(jax.random.fold_in(streams_of[3], 3), SECTIONS * TOKENS // TOK_DEV)
    expert_ids = jax.vmap(lambda own, number: shared_out(jax.random.fold_in(streams_of[3], 2), own, number, TOK_DEV, ALL_EXPERTS, TOP, CAP, 2))(expert_ids_keys, expert_ids_turns).reshape((SECTIONS, TOKENS, TOP))
    combine = jnp.clip(0.049804688 + 0.24902344 * jax.random.uniform(streams_of[4], (SECTIONS, TOKENS, TOP), jnp.float32) ** block_levels(streams_of[4], (SECTIONS, TOKENS, TOP), ((0, 8), (1, 64)), -0.2, 0.2), 0.049804688, 0.29882812).astype(jnp.bfloat16)
    w_gate = scatter_about(streams_of[5], (SECTIONS, EXPERTS * FFE, D), D ** -0.5, 0.125, ((0, 8), (1, 64)))
    w_up = scatter_about(streams_of[6], (SECTIONS, EXPERTS * FFE, D), D ** -0.5, 0.125, ((0, 8), (1, 64)))
    w_down = scatter_about(streams_of[7], (SECTIONS, EXPERTS * FFE, D), FFE ** -0.5, 0.21875, ((0, 8), (1, 64)))
    return {"layer_input": layer_input, "out_grad": out_grad, "norm_gain": norm_gain, "expert_ids": expert_ids, "combine": combine, "w_gate": w_gate, "w_up": w_up, "w_down": w_down}


epsilon = 1e-06

def contract_cols(left, right):
    return lax.dot_general(left, right, (((1,), (1,)), ((), ())), preferred_element_type=jnp.float32)

def expert_block(rows_x, rows_dy, rows_w, weight_gate, weight_up, weight_down):
    slice_units = FFE // SPLIT
    gate = contract_cols(rows_x, weight_gate)
    upper = contract_cols(rows_x, weight_up)
    sigma = jax.nn.sigmoid(gate)
    active = gate * sigma
    hidden = (active * upper).astype(jnp.bfloat16)
    hidden_s = hidden.astype(jnp.float32).reshape(-1, SPLIT, slice_units)
    down_s = weight_down.astype(jnp.float32).reshape(SPLIT, slice_units, D)
    output_s = jnp.einsum('rsf,sfd->rsd', hidden_s, down_s)
    comb_s = lax.optimization_barrier(jnp.sum(rows_dy.astype(jnp.float32)[:, None, :] * output_s, axis=-1)).astype(jnp.bfloat16)
    comb_part = lax.optimization_barrier(jnp.sum(comb_s.astype(jnp.float32), axis=1)).astype(jnp.bfloat16)
    scaled = (rows_w.astype(jnp.float32)[:, None] * rows_dy.astype(jnp.float32)).astype(jnp.bfloat16)
    hidden_grad = contract_cols(scaled, weight_down)
    gate_part = (hidden_grad * upper * sigma * (1.0 + gate * (1.0 - sigma))).astype(jnp.bfloat16)
    up_part = (hidden_grad * active).astype(jnp.bfloat16)
    gate_ps = gate_part.astype(jnp.float32).reshape(-1, SPLIT, slice_units)
    up_ps = up_part.astype(jnp.float32).reshape(-1, SPLIT, slice_units)
    wg_s = weight_gate.astype(jnp.float32).reshape(SPLIT, slice_units, D)
    wu_s = weight_up.astype(jnp.float32).reshape(SPLIT, slice_units, D)
    route_s = (jnp.einsum('rsf,sfd->rsd', gate_ps, wg_s) + jnp.einsum('rsf,sfd->rsd', up_ps, wu_s)).astype(jnp.bfloat16)
    rows_grad = lax.optimization_barrier(jnp.sum(route_s.astype(jnp.float32), axis=1))
    return (rows_grad, comb_part)

def section_grads(inputs, incoming_gradient, scale_factors, choices, weights, weight_gate, weight_up, weight_down):
    routes = TOK_DEV * TOP
    float_values = inputs.astype(jnp.float32)
    reciprocal_norm = lax.rsqrt(lax.optimization_barrier(jnp.mean(float_values * float_values, axis=-1, keepdims=True)) + epsilon)
    normalized_rows = float_values * reciprocal_norm
    normalized_input = (normalized_rows * scale_factors[None, :]).astype(jnp.bfloat16)
    ids_dev = choices.reshape(N_EXPERT, routes)
    onehot = (ids_dev[:, :, None] == jnp.arange(EXPERTS, dtype=jnp.int32)[None, None, :]).astype(jnp.int32)
    before = jnp.cumsum(onehot, axis=1) - onehot
    slot = lax.optimization_barrier(jnp.sum(before * onehot, axis=-1)).astype(jnp.int32)
    route_ids = jnp.arange(N_EXPERT * routes, dtype=jnp.int32).reshape(N_EXPERT, routes)
    source = jnp.broadcast_to(jnp.arange(N_EXPERT, dtype=jnp.int32)[:, None], (N_EXPERT, routes))
    table = jnp.full((EXPERTS, N_EXPERT, CAP), N_EXPERT * routes, jnp.int32)
    table = table.at[ids_dev, source, slot].set(route_ids, mode='drop')
    flat_route = table.reshape(EXPERTS, N_EXPERT * CAP)
    normed_ext = jnp.concatenate([normalized_input, jnp.zeros((1, D), jnp.bfloat16)], axis=0)
    upstream_ext = jnp.concatenate([incoming_gradient, jnp.zeros((1, D), jnp.bfloat16)], axis=0)
    weight_ext = jnp.concatenate([weights.reshape(-1), jnp.zeros((1,), jnp.bfloat16)], axis=0)
    gate_e = weight_gate.reshape(EXPERTS, FFE, D)
    up_e = weight_up.reshape(EXPERTS, FFE, D)
    down_e = weight_down.reshape(EXPERTS, FFE, D)

    def per_expert(items):
        index, gate_w, up_w, down_w = items
        token = index // TOP
        return expert_block(normed_ext[token], upstream_ext[token], weight_ext[index], gate_w, up_w, down_w)
    rows_grad, comb_part = lax.map(per_expert, (flat_route, gate_e, up_e, down_e))
    all_index = flat_route.reshape(-1)
    normalized_gradient = jnp.zeros((TOKENS + 1, D), jnp.float32).at[all_index // TOP].add(rows_grad.reshape(-1, D))[:TOKENS]
    comb_out = jnp.zeros((N_EXPERT * routes + 1,), jnp.bfloat16).at[all_index].set(comb_part.reshape(-1))[:N_EXPERT * routes].reshape(TOKENS, TOP)
    gain_product = lax.optimization_barrier(jnp.sum(normalized_gradient * normalized_rows, axis=0))
    scaled_gradient = normalized_gradient * scale_factors[None, :]
    inner_product = lax.optimization_barrier(jnp.mean(scaled_gradient * normalized_rows, axis=-1, keepdims=True))
    input_gradient = (incoming_gradient.astype(jnp.float32) + reciprocal_norm * (scaled_gradient - normalized_rows * inner_product)).astype(jnp.bfloat16)
    return (input_gradient, comb_out, gain_product)

def reference(layer_input, out_grad, norm_gain, expert_ids, combine, w_gate, w_up, w_down):
    results = [section_grads(layer_input[level], out_grad[level], norm_gain[level], expert_ids[level], combine[level], w_gate[level], w_up[level], w_down[level]) for level in range(SECTIONS)]
    input_grads = jnp.stack([item[0] for item in results])
    passed_grad = jnp.concatenate([input_grads[1:], jnp.zeros((1, TOKENS, D), jnp.bfloat16)], axis=0)
    comb_grad = jnp.stack([item[1] for item in results])
    gain_grad = jnp.stack([item[2] for item in results])
    return (passed_grad, comb_grad, gain_grad)
```

```python
import jax
import jax.numpy as jnp
from jax import lax
from jax.experimental import pallas as pl
from jax.experimental.pallas import tpu as pltpu
from jax.sharding import PartitionSpec as P

MESH = pl.DeviceIdType.MESH
NX, NZ = 4, 8
CAP = 8
D = 2048
HALF = D // 2
HID = 192
TOK = 64
TOP = 8
BACK = HALF + 128
EPS = 1e-06
F32, BF16 = jnp.float32, jnp.bfloat16


def nt(left, right):
    return lax.dot_general(left, right, (((1,), (1,)), ((), ())), preferred_element_type=F32)


def nn(left, right):
    return jnp.dot(left, right, preferred_element_type=F32)


def kernel(
    x_ref, dy_ref, g_ref, ids_ref, cw_ref, wg_ref, wu_ref, wd_ref,
    passed_ref, comb_ref, gain_ref,
    send, recv, w, ret, got, grads, sum_xc, sum_z,
    disp_sem, recv_sem, fwd_sem, ret_sem, got_sem, wl_sem, ws_sem, wr_sem,
    xs_sem, xr_sem, zs_sem, zr_sem, pass_sem,
):
    sec = lax.axis_index("section")
    me = lax.axis_index("expert")
    core = lax.rem(me, 2)
    z = lax.rem(me // 2, NZ)
    x = me // (2 * NZ)
    way = 1 - 2 * lax.rem(z, 2)
    mate_z = z + way

    def place(px, pz, pc):
        return (sec, (lax.rem(px + NX, NX) * NZ + lax.rem(pz + 2 * NZ, NZ)) * 2 + pc)

    def entry_z(d):
        return z + way * d if d % 2 == 0 else z - way * d

    sibling = place(x, z, 1 - core)
    mate = place(x, mate_z, core)
    ahead = (lax.rem(sec + 7, 8), me)
    behind = (lax.rem(sec + 1, 8), me)

    barrier = pltpu.get_barrier_semaphore()

    def greet(q, carry):
        chip = lax.rem(x * NZ + z + q, NX * NZ)
        pl.semaphore_signal(barrier, inc=1, device_id=(sec, chip * 2 + core), device_id_type=MESH)
        return carry

    lax.fori_loop(1, NX * NZ, greet, 0)
    for q in range(NX):
        pl.semaphore_signal(
            barrier, inc=1, device_id=place(x + q, z, 1 - core), device_id_type=MESH
        )
    for other in (ahead, behind):
        pl.semaphore_signal(barrier, inc=1, device_id=other, device_id_type=MESH)

    own = []
    for n, ref in enumerate((wg_ref, wu_ref, wd_ref)):
        copy = pltpu.make_async_copy(ref, w.at[2 * n], wl_sem.at[n])
        copy.start()
        own.append(copy)

    rows = x_ref[...].astype(F32)
    rinv = lax.rsqrt(jnp.mean(rows * rows, axis=-1, keepdims=True) + EPS)
    normed = (rows * rinv * g_ref[...]).astype(BF16)
    dy = dy_ref[...]
    ids = ids_ref[...]
    weights = cw_ref[...].astype(F32)

    def expert_of(block):
        d, dx = block // 4, lax.rem(block, 4)
        ez = jnp.where(lax.rem(d, 2) == 0, z + way * d, z - way * d)
        ez = lax.rem(ez + 2 * NZ, NZ)
        return lax.rem(x + dx, NX) * 4 + ez // 2

    before = (
        lax.broadcasted_iota(jnp.int32, (TOK, TOK), 0)
        > lax.broadcasted_iota(jnp.int32, (TOK, TOK), 1)
    ).astype(BF16)

    def picks(lanes, per):
        lane = lax.broadcasted_iota(jnp.int32, (TOK, lanes), 1)
        expert = expert_of(lane // per)
        named = jnp.zeros((TOK, lanes), F32)
        scaled = jnp.zeros((TOK, lanes), F32)
        for k in range(TOP):
            hit = ids[:, k : k + 1] == expert
            named = jnp.where(hit, 1.0, named)
            scaled = jnp.where(hit, weights[:, k : k + 1], scaled)
        rank = nn(before, named.astype(BF16))
        mine = rank == lax.rem(lane, CAP).astype(F32)
        return lane, expert, jnp.where(mine, named, 0.0), jnp.where(mine, scaled, 0.0)

    _, _, token_pick, _ = picks(128, CAP)
    pick = token_pick.astype(BF16)

    def tn(left, right):
        return lax.dot_general(left, right, (((0,), (0,)), ((), ())), preferred_element_type=F32)

    for c in range(4):
        cols = slice(c * 512, (c + 1) * 512)
        part_x = tn(pick, normed[:, cols]).reshape(16, CAP, 512)
        part_dy = tn(pick, dy[:, cols]).reshape(16, CAP, 512)
        send[:, :, cols] = jnp.concatenate([part_x, part_dy], axis=1).astype(BF16)
    recv[0, 0] = send[0]

    pl.semaphore_wait(barrier, NX * NZ - 1 + NX + 2)

    def dispatch(d, dx):
        return pltpu.make_async_remote_copy(
            src_ref=send.at[d * 4 + dx],
            dst_ref=recv.at[d, dx],
            send_sem=disp_sem.at[d * 4 + dx],
            recv_sem=recv_sem.at[d * 4 + dx],
            device_id=place(x + dx, entry_z(d), core),
            device_id_type=MESH,
        )

    def hand_on(d, dx):
        return pltpu.make_async_remote_copy(
            src_ref=recv.at[d, dx],
            dst_ref=recv.at[d + 4, dx],
            send_sem=fwd_sem.at[d * 4 + dx],
            recv_sem=recv_sem.at[16 + d * 4 + dx],
            device_id=mate,
            device_id_type=MESH,
        )

    def weight_swap(n, ref):
        return pltpu.make_async_remote_copy(
            src_ref=ref,
            dst_ref=w.at[2 * n + 1],
            send_sem=ws_sem.at[n],
            recv_sem=wr_sem.at[n],
            device_id=sibling,
            device_id_type=MESH,
        )

    hand_on(0, 0).start()
    for d in range(4):
        for dx in range(NX):
            if (d, dx) != (0, 0):
                dispatch(d, dx).start()
    swaps = [weight_swap(n, ref) for n, ref in enumerate((wg_ref, wu_ref, wd_ref))]
    for copy in swaps:
        copy.start()
    for copy in own:
        copy.wait()
    for copy in swaps:
        copy.wait()

    def giveback(g, dx):
        direct = g < 4
        d = jnp.where(direct, g, g - 4)
        pz = jnp.where(direct, z - way * d, mate_z + way * d)
        return pltpu.make_async_remote_copy(
            src_ref=ret.at[g * 4 + dx],
            dst_ref=got.at[g * 4 + dx],
            send_sem=ret_sem.at[g * 4 + dx],
            recv_sem=got_sem.at[g * 4 + dx],
            device_id=place(x - dx, pz, core),
            device_id_type=MESH,
        )

    def group(g, carry):
        for dx in range(NX):

            def arrived(dx=dx):
                pltpu.make_async_copy(
                    recv.at[g, dx], recv.at[g, dx], recv_sem.at[g * 4 + dx]
                ).wait()

            if dx == 0:
                pl.when(g > 0)(arrived)
            else:
                arrived()

            @pl.when((g < 4) if dx else ((g > 0) & (g < 4)))
            def _(dx=dx):
                hand_on(g, dx).start()

        block = recv[g].reshape(4 * 16, D)
        gate = nt(block, w[0:2].reshape(2 * HID, D)).reshape(4, 16, 2 * HID)[:, :8]
        upper = nt(block, w[2:4].reshape(2 * HID, D)).reshape(4, 16, 2 * HID)[:, :8]
        down = nt(block, w[4:6].reshape(2 * HID, D)).reshape(4, 16, 2 * HID)[:, 8:]
        sigma = jax.nn.sigmoid(gate)
        active = gate * sigma
        hidden = (active * upper).astype(BF16).astype(F32)
        comb = jnp.sum(hidden * down, axis=-1, keepdims=True)
        gate_part = down * upper * sigma * (1.0 + gate * (1.0 - sigma))
        gate_part = gate_part.reshape(4 * 8, 2 * HID).astype(BF16)
        up_part = (down * active).reshape(4 * 8, 2 * HID).astype(BF16)
        halves = []
        for c in range(2):
            cols = slice(c * HALF, (c + 1) * HALF)
            part = nn(gate_part, w[0:2, :, cols].reshape(2 * HID, HALF))
            part += nn(up_part, w[2:4, :, cols].reshape(2 * HID, HALF))
            halves.append(part.reshape(4, 8, HALF))
        out = jnp.concatenate(halves, axis=1).astype(BF16)
        comb = jnp.broadcast_to(comb, (4, 8, 128))
        comb = jnp.concatenate([comb, jnp.zeros((4, 8, 128), F32)], axis=1).astype(BF16)
        for dx in range(NX):
            ret[g * 4 + dx, :, 0:HALF] = out[dx]
            ret[g * 4 + dx, :, HALF:BACK] = comb[dx]
        for dx in range(NX):
            if dx == 0:

                @pl.when(g == 0)
                def _():
                    got[0] = ret[0]

                @pl.when(g > 0)
                def _():
                    giveback(g, 0).start()
            else:
                giveback(g, dx).start()
        return carry

    lax.fori_loop(0, 8, group, 0)

    lane, expert, chosen, scaled = picks(256, 16)
    first = lax.rem(lane, 16) < 8
    low = jnp.where(first, scaled, 0.0).astype(BF16)
    high = jnp.where(first, 0.0, scaled).astype(BF16)
    chosen = jnp.where(first, chosen, 0.0)

    for n in range(1, 32):
        pltpu.make_async_copy(got.at[n], got.at[n], got_sem.at[n]).wait()

    back = [got[h * 16 : (h + 1) * 16, :, 0:HALF].reshape(256, HALF) for h in range(2)]
    total = [nn(side, back[0]) + nn(side, back[1]) for side in (low, high)]

    mean = jnp.zeros((TOK, 1), F32)
    for c in range(2):
        cols = slice(c * HALF, (c + 1) * HALF)
        hat = x_ref[:, cols].astype(F32) * rinv
        product = total[c] * hat
        sum_xc[x * 2 + core, :, cols] = jnp.sum(product, axis=0, keepdims=True)
        mean += jnp.sum(product * g_ref[:, cols], axis=-1, keepdims=True)
    mean = mean / D

    def share_xc(dx, dc):
        return pltpu.make_async_remote_copy(
            src_ref=sum_xc.at[x * 2 + core],
            dst_ref=sum_xc.at[x * 2 + core],
            send_sem=xs_sem.at[dx * 2 + dc],
            recv_sem=xr_sem.at[dx * 2 + dc],
            device_id=place(x + dx, z, lax.rem(core + dc, 2)),
            device_id_type=MESH,
        )

    others = [(dx, dc) for dx in range(NX) for dc in range(2) if (dx, dc) != (0, 0)]
    for dx, dc in others:
        share_xc(dx, dc).start()

    for c in range(2):
        cols = slice(c * HALF, (c + 1) * HALF)
        hat = x_ref[:, cols].astype(F32) * rinv
        grad = dy_ref[:, cols].astype(F32) + rinv * (total[c] * g_ref[:, cols] - hat * mean)
        grads[:, cols] = grad.astype(BF16)

    def pass_on():
        return pltpu.make_async_remote_copy(
            src_ref=grads,
            dst_ref=passed_ref,
            send_sem=pass_sem.at[0],
            recv_sem=pass_sem.at[1],
            device_id=ahead,
            device_id_type=MESH,
        )

    @pl.when(sec > 0)
    def _():
        pass_on().start()

    comb_back = [got[h * 16 : (h + 1) * 16, :, HALF:BACK].reshape(256, 128) for h in range(2)]
    column = lax.broadcasted_iota(jnp.int32, (TOK, 128), 1)
    comb = jnp.zeros((TOK, 128), F32)
    for k in range(TOP):
        one = jnp.where(ids[:, k : k + 1] == expert, chosen, 0.0).astype(BF16)
        comb = jnp.where(column == k, nn(one, comb_back[0]) + nn(one, comb_back[1]), comb)
    comb_ref[...] = comb[:, 0:TOP].astype(BF16)

    for dx, dc in others:
        share_xc(dx, dc).wait()
    sum_z[z] = jnp.sum(sum_xc[...], axis=0)

    def share_z(dz):
        return pltpu.make_async_remote_copy(
            src_ref=sum_z.at[z],
            dst_ref=sum_z.at[z],
            send_sem=zs_sem.at[dz],
            recv_sem=zr_sem.at[dz],
            device_id=place(x, z + dz, core),
            device_id_type=MESH,
        )

    for dz in range(1, NZ):
        share_z(dz).start()

    for d in range(4):
        for dx in range(NX):
            if (d, dx) != (0, 0):
                dispatch(d, dx).wait_send()
            hand_on(d, dx).wait_send()

    def sent(n, carry):
        pltpu.make_async_copy(ret.at[n], ret.at[n], ret_sem.at[n]).wait()
        return carry

    lax.fori_loop(1, 32, sent, 0)
    for dz in range(1, NZ):
        share_z(dz).wait()
    gain_ref[...] = jnp.sum(sum_z[...], axis=0)

    @pl.when(sec > 0)
    def _():
        pass_on().wait_send()

    @pl.when(sec < 7)
    def _():
        pass_on().wait_recv()

    @pl.when(sec == 7)
    def _():
        grads[...] = jnp.zeros_like(grads)
        clear = pltpu.make_async_copy(grads, passed_ref, pass_sem.at[1])
        clear.start()
        clear.wait()


def per_device(layer_input, out_grad, norm_gain, expert_ids, combine, w_gate, w_up, w_down):
    vmem = pl.BlockSpec(memory_space=pltpu.VMEM)
    hbm = pl.BlockSpec(memory_space=pl.ANY)
    dma = pltpu.SemaphoreType.DMA
    passed, comb, gain = pl.pallas_call(
        kernel,
        out_shape=(
            jax.ShapeDtypeStruct((TOK, D), BF16),
            jax.ShapeDtypeStruct((TOK, TOP), BF16),
            jax.ShapeDtypeStruct((1, D), F32),
        ),
        in_specs=[vmem] * 5 + [hbm] * 3,
        out_specs=(hbm, vmem, vmem),
        scratch_shapes=[
            pltpu.VMEM((16, 16, D), BF16),
            pltpu.VMEM((8, NX, 16, D), BF16),
            pltpu.VMEM((6, HID, D), BF16),
            pltpu.VMEM((32, 16, BACK), BF16),
            pltpu.VMEM((32, 16, BACK), BF16),
            pltpu.VMEM((TOK, D), BF16),
            pltpu.VMEM((8, 1, D), F32),
            pltpu.VMEM((8, 1, D), F32),
            dma((16,)), dma((32,)), dma((16,)), dma((32,)), dma((32,)),
            dma((3,)), dma((3,)), dma((3,)),
            dma((8,)), dma((8,)), dma((8,)), dma((8,)), dma((2,)),
        ],
        compiler_params=pltpu.CompilerParams(
            collective_id=0, has_side_effects=True, vmem_limit_bytes=48 * 1024 * 1024
        ),
    )(
        layer_input[0], out_grad[0], norm_gain, expert_ids[0], combine[0],
        w_gate[0], w_up[0], w_down[0],
    )
    return passed[None], comb[None], gain


def solution(mesh):
    rows = P("section", "expert", None)
    whole = P("section", None)
    return jax.shard_map(
        per_device,
        mesh=mesh,
        in_specs=(rows, rows, whole, rows, rows, rows, rows, rows),
        out_specs=(rows, rows, whole),
        check_vma=False,
    )
```

```python
import jax
import jax.numpy as jnp
from jax import lax
from jax.experimental import pallas as pl
from jax.experimental.pallas import tpu as pltpu
from jax.sharding import PartitionSpec as P

MESH = pl.DeviceIdType.MESH
NX, NZ = 4, 8
CAP = 8
D = 2048
HALF = D // 2
HID = 192
TOK = 64
TOP = 8
BACK = HALF + 128
EPS = 1e-06
F32, BF16 = jnp.float32, jnp.bfloat16


def nt(left, right):
    return lax.dot_general(left, right, (((1,), (1,)), ((), ())), preferred_element_type=F32)


def nn(left, right):
    return jnp.dot(left, right, preferred_element_type=F32)


def kernel(
    x_hbm, dy_hbm, g_hbm, ids_hbm, cw_hbm, wg_ref, wu_ref, wd_ref,
    passed_ref, comb_ref, gain_ref,
    x_ref, dy_ref, g_ref, ids_ref, cw_ref,
    send, recv, w, ret, got, hold, part, grads, gain_sum, sum_xc, sum_z,
    in_sem, disp_sem, recv_sem, fwd_sem, ret_sem, got_sem, part_sem, wl_sem, ws_sem, wr_sem,
    xs_sem, xr_sem, zs_sem, zr_sem, pass_sem,
):
    sec = lax.axis_index("section")
    me = lax.axis_index("expert")
    core = lax.rem(me, 2)
    z = lax.rem(me // 2, NZ)
    x = me // (2 * NZ)
    way = 1 - 2 * lax.rem(z, 2)
    mate_z = z + way

    def place(px, pz, pc):
        return (sec, (lax.rem(px + NX, NX) * NZ + lax.rem(pz + 2 * NZ, NZ)) * 2 + pc)

    def entry_z(d):
        return z + way * d if d % 2 == 0 else z - way * d

    sibling = place(x, z, 1 - core)
    mate = place(x, mate_z, core)
    ahead = (lax.rem(sec + 7, 8), me)
    behind = (lax.rem(sec + 1, 8), me)

    fetch = []
    pairs = ((x_hbm, x_ref), (g_hbm, g_ref), (ids_hbm, ids_ref), (cw_hbm, cw_ref), (dy_hbm, dy_ref))
    for n, (src, dst) in enumerate(pairs):
        copy = pltpu.make_async_copy(src, dst, in_sem.at[n])
        copy.start()
        fetch.append(copy)

    barrier = pltpu.get_barrier_semaphore()

    def greet(q, carry):
        chip = lax.rem(x * NZ + z + q, NX * NZ)
        pl.semaphore_signal(barrier, inc=1, device_id=(sec, chip * 2 + core), device_id_type=MESH)
        return carry

    lax.fori_loop(1, NX * NZ, greet, 0)
    for q in range(NX):
        pl.semaphore_signal(
            barrier, inc=1, device_id=place(x + q, z, 1 - core), device_id_type=MESH
        )
    for other in (ahead, behind):
        pl.semaphore_signal(barrier, inc=1, device_id=other, device_id_type=MESH)

    own = []
    for n, ref in enumerate((wg_ref, wu_ref, wd_ref)):
        copy = pltpu.make_async_copy(ref, w.at[2 * n], wl_sem.at[n])
        copy.start()
        own.append(copy)

    for copy in fetch:
        copy.wait()

    rows = x_ref[...].astype(F32)
    rinv = lax.rsqrt(jnp.mean(rows * rows, axis=-1, keepdims=True) + EPS)
    normed = (rows * rinv * g_ref[...]).astype(BF16)
    dy = dy_ref[...]
    ids = ids_ref[...]
    weights = cw_ref[...].astype(F32)

    def expert_of(block):
        d, dx = block // 4, lax.rem(block, 4)
        ez = jnp.where(lax.rem(d, 2) == 0, z + way * d, z - way * d)
        ez = lax.rem(ez + 2 * NZ, NZ)
        return lax.rem(x + dx, NX) * 4 + ez // 2

    before = (
        lax.broadcasted_iota(jnp.int32, (TOK, TOK), 0)
        < lax.broadcasted_iota(jnp.int32, (TOK, TOK), 1)
    ).astype(BF16)

    def picks(slots, per):
        slot = lax.broadcasted_iota(jnp.int32, (slots, TOK), 0)
        expert = expert_of(slot // per)
        named = jnp.zeros((slots, TOK), F32)
        scaled = jnp.zeros((slots, TOK), F32)
        for k in range(TOP):
            hit = ids[k : k + 1, :] == expert
            named = jnp.where(hit, 1.0, named)
            scaled = jnp.where(hit, weights[k : k + 1, :], scaled)
        rank = nn(named.astype(BF16), before)
        mine = rank == lax.rem(slot, CAP).astype(F32)
        return slot, expert, jnp.where(mine, named, 0.0), jnp.where(mine, scaled, 0.0)

    _, _, token_pick, scaled_pick = picks(128, CAP)
    token_pick, scaled_pick = token_pick.astype(BF16), scaled_pick.astype(BF16)

    def tn(left, right):
        return lax.dot_general(left, right, (((0,), (0,)), ((), ())), preferred_element_type=F32)

    for c in range(4):
        cols = slice(c * 512, (c + 1) * 512)
        part_x = nn(token_pick, normed[:, cols]).reshape(16, CAP, 512)
        part_dy = nn(scaled_pick, dy[:, cols]).reshape(16, CAP, 512)
        send[:, :, cols] = jnp.concatenate([part_x, part_dy], axis=1).astype(BF16)
    recv[0, 0] = send[0]

    pl.semaphore_wait(barrier, NX * NZ - 1 + NX + 2)

    def dispatch(d, dx):
        return pltpu.make_async_remote_copy(
            src_ref=send.at[d * 4 + dx],
            dst_ref=recv.at[d, dx],
            send_sem=disp_sem.at[d * 4 + dx],
            recv_sem=recv_sem.at[d * 4 + dx],
            device_id=place(x + dx, entry_z(d), core),
            device_id_type=MESH,
        )

    def hand_on(d, dx):
        return pltpu.make_async_remote_copy(
            src_ref=recv.at[d, dx],
            dst_ref=recv.at[d + 4, dx],
            send_sem=fwd_sem.at[d * 4 + dx],
            recv_sem=recv_sem.at[16 + d * 4 + dx],
            device_id=mate,
            device_id_type=MESH,
        )

    def weight_swap(n, ref):
        return pltpu.make_async_remote_copy(
            src_ref=ref,
            dst_ref=w.at[2 * n + 1],
            send_sem=ws_sem.at[n],
            recv_sem=wr_sem.at[n],
            device_id=sibling,
            device_id_type=MESH,
        )

    hand_on(0, 0).start()
    swaps = [weight_swap(n, ref) for n, ref in enumerate((wg_ref, wu_ref, wd_ref))]
    for d in range(4):
        for dx in range(NX):
            if (d, dx) != (0, 0):
                dispatch(d, dx).start()
    for copy in swaps:
        copy.start()

    def landed(buffer, semaphore):
        pltpu.make_async_copy(buffer, buffer, semaphore).wait()

    def forward(d):
        for dx in range(NX):
            if (d, dx) != (0, 0):
                landed(recv.at[d, dx], recv_sem.at[d * 4 + dx])
                hand_on(d, dx).start()

    def giveback(g, dx):
        direct = g < 4
        d = jnp.where(direct, g, g - 4)
        pz = jnp.where(direct, z - way * d, mate_z + way * d)
        return pltpu.make_async_remote_copy(
            src_ref=ret.at[g * 4 + dx],
            dst_ref=got.at[g * 4 + dx],
            send_sem=ret_sem.at[g * 4 + dx],
            recv_sem=got_sem.at[g * 4 + dx],
            device_id=place(x - dx, pz, core),
            device_id_type=MESH,
        )

    def halfway(g, dx):
        return pltpu.make_async_remote_copy(
            src_ref=ret.at[g * 4 + dx],
            dst_ref=part.at[(g - 6) * 4 + dx],
            send_sem=ret_sem.at[g * 4 + dx],
            recv_sem=part_sem.at[(g - 6) * 4 + dx],
            device_id=mate,
            device_id_type=MESH,
        )

    def join(d):
        for dx in range(NX):
            n = (d - 2) * 4 + dx
            landed(part.at[n], part_sem.at[n])
            ret[d * 4 + dx] = (hold[n] + part[n].astype(F32)).astype(BF16)
            giveback(d, dx).start()

    forward(0)
    forward(1)
    for copy in own:
        copy.wait()
    for copy in swaps:
        copy.wait()

    gain_sum[...] = jnp.zeros_like(gain_sum)
    order = (0, 1, 4, 2, 5, 3, 6, 7)

    def group(i, carry):
        g = jnp.int32(order[0])
        for n in range(1, 8):
            g = jnp.where(i == n, order[n], g)

        @pl.when(i == 1)
        def _():
            forward(2)

        @pl.when(i == 2)
        def _():
            forward(3)

        @pl.when(g >= 4)
        def _():
            for dx in range(NX):
                landed(recv.at[g, dx], recv_sem.at[g * 4 + dx])

        block = recv[g].reshape(4 * 16, D)
        gate = nt(block, w[0:2].reshape(2 * HID, D)).reshape(4, 16, 2 * HID)[:, :8]
        upper = nt(block, w[2:4].reshape(2 * HID, D)).reshape(4, 16, 2 * HID)[:, :8]
        down = nt(block, w[4:6].reshape(2 * HID, D)).reshape(4, 16, 2 * HID)[:, 8:]
        sigma = jax.nn.sigmoid(gate)
        active = gate * sigma
        hidden = (active * upper).astype(BF16).astype(F32)
        comb = jnp.sum(hidden * down, axis=-1, keepdims=True)
        gate_part = down * upper * sigma * (1.0 + gate * (1.0 - sigma))
        gate_part = gate_part.reshape(4 * 8, 2 * HID).astype(BF16)
        up_part = (down * active).reshape(4 * 8, 2 * HID).astype(BF16)
        halves = []
        for c in range(2):
            cols = slice(c * HALF, (c + 1) * HALF)
            piece = nn(gate_part, w[0:2, :, cols].reshape(2 * HID, HALF))
            piece += nn(up_part, w[2:4, :, cols].reshape(2 * HID, HALF))
            piece = piece.reshape(4, 8, HALF)
            halves.append(piece)
            held = recv[g, :, :, cols].astype(F32)[:, :8]
            gain_sum[:, cols] += jnp.sum(piece * held, axis=0)
        out = jnp.concatenate(halves, axis=1)
        comb = jnp.broadcast_to(comb, (4, 8, 128))
        comb = jnp.concatenate([comb, jnp.zeros((4, 8, 128), F32)], axis=1)
        kept = (g == 2) | (g == 3)
        half = (g == 6) | (g == 7)

        @pl.when(kept)
        def _():
            for dx in range(NX):
                hold[(g - 2) * 4 + dx, :, 0:HALF] = out[dx]
                hold[(g - 2) * 4 + dx, :, HALF:BACK] = comb[dx]

        @pl.when(jnp.logical_not(kept))
        def _():
            for dx in range(NX):
                ret[g * 4 + dx, :, 0:HALF] = out[dx].astype(BF16)
                ret[g * 4 + dx, :, HALF:BACK] = comb[dx].astype(BF16)

        @pl.when(half)
        def _():
            for dx in range(NX):
                halfway(g, dx).start()

        @pl.when(jnp.logical_not(kept | half))
        def _():
            for dx in range(NX):
                if dx == 0:

                    @pl.when(g == 0)
                    def _():
                        got[0] = ret[0]

                    @pl.when(g > 0)
                    def _():
                        giveback(g, 0).start()
                else:
                    giveback(g, dx).start()

        return carry

    lax.fori_loop(0, 8, group, 0)

    sum_xc[x * 2 + core] = jnp.sum(gain_sum[...], axis=0, keepdims=True)

    def share_xc(dx, dc):
        return pltpu.make_async_remote_copy(
            src_ref=sum_xc.at[x * 2 + core],
            dst_ref=sum_xc.at[x * 2 + core],
            send_sem=xs_sem.at[dx * 2 + dc],
            recv_sem=xr_sem.at[dx * 2 + dc],
            device_id=place(x + dx, z, lax.rem(core + dc, 2)),
            device_id_type=MESH,
        )

    others = [(dx, dc) for dx in range(NX) for dc in range(2) if (dx, dc) != (0, 0)]
    for dx, dc in others:
        share_xc(dx, dc).start()

    join(2)
    join(3)

    for dx, dc in others:
        share_xc(dx, dc).wait()
    sum_z[z] = jnp.sum(sum_xc[...], axis=0)

    def share_z(dz):
        return pltpu.make_async_remote_copy(
            src_ref=sum_z.at[z],
            dst_ref=sum_z.at[z],
            send_sem=zs_sem.at[dz],
            recv_sem=zr_sem.at[dz],
            device_id=place(x, z + dz, core),
            device_id_type=MESH,
        )

    for dz in range(1, NZ):
        share_z(dz).start()

    slot, expert, chosen, _ = picks(256, 16)
    first = lax.rem(slot, 16) < 8
    low = jnp.where(first, chosen, 0.0).astype(BF16)
    high = jnp.where(first, 0.0, chosen).astype(BF16)
    chosen = jnp.where(first, chosen, 0.0)

    for n in [1, 2, 3, 4, 5, 6, 7, 8, 9, 10, 11, 12, 13, 14, 15, 16, 17, 18, 19, 20, 21, 22, 23]:
        landed(got.at[n], got_sem.at[n])

    spans = [(0, 16, 0), (16, 24, 0)]
    total = []
    for side in (low, high):
        sums = 0.0
        for lo, hi, at in spans:
            size = (hi - lo) * 16
            sums += tn(side[at : at + size], got[lo:hi, :, 0:HALF].reshape(size, HALF))
        total.append(sums)

    hats = [x_ref[:, c * HALF : (c + 1) * HALF].astype(F32) * rinv for c in range(2)]
    products = [total[c] * hats[c] for c in range(2)]
    mean = 0.0
    for c in range(2):
        cols = slice(c * HALF, (c + 1) * HALF)
        mean += jnp.sum(products[c] * g_ref[:, cols], axis=-1, keepdims=True)
    mean = mean / D
    for c in range(2):
        cols = slice(c * HALF, (c + 1) * HALF)
        scaled_grad = total[c] * g_ref[:, cols]
        grad = dy_ref[:, cols].astype(F32) + rinv * (scaled_grad - hats[c] * mean)
        grads[:, cols] = grad.astype(BF16)

    def pass_on():
        return pltpu.make_async_remote_copy(
            src_ref=grads,
            dst_ref=passed_ref,
            send_sem=pass_sem.at[0],
            recv_sem=pass_sem.at[1],
            device_id=ahead,
            device_id_type=MESH,
        )

    @pl.when(sec > 0)
    def _():
        pass_on().start()

    line = lax.broadcasted_iota(jnp.int32, (TOP, TOK), 0)
    comb = jnp.zeros((TOP, TOK), F32)
    found = got[0:16, :, HALF:BACK].astype(F32).reshape(256, 128)[:, 0:TOK]
    extra = got[16:24, :, HALF:BACK].astype(F32).reshape(128, 128)[:, 0:TOK]
    found = chosen * jnp.concatenate([found[0:128] + extra, found[128:256]], axis=0)
    for k in range(TOP):
        one = jnp.where(ids[k : k + 1, :] == expert, found, 0.0)
        comb = jnp.where(line == k, jnp.sum(one, axis=0, keepdims=True), comb)
    comb_ref[...] = (comb / weights).astype(BF16)

    for d in range(4):
        for dx in range(NX):
            if (d, dx) != (0, 0):
                dispatch(d, dx).wait_send()
            hand_on(d, dx).wait_send()

    def sent(n, carry):
        landed(ret.at[n], ret_sem.at[n])
        return carry

    lax.fori_loop(1, 32, sent, 0)
    for dz in range(1, NZ):
        share_z(dz).wait()
    gain_ref[...] = jnp.sum(sum_z[...], axis=0) / g_ref[...]

    @pl.when(sec > 0)
    def _():
        pass_on().wait_send()

    @pl.when(sec < 7)
    def _():
        pass_on().wait_recv()

    @pl.when(sec == 7)
    def _():
        grads[...] = jnp.zeros_like(grads)
        clear = pltpu.make_async_copy(grads, passed_ref, pass_sem.at[1])
        clear.start()
        clear.wait()


def per_device(layer_input, out_grad, norm_gain, expert_ids, combine, w_gate, w_up, w_down):
    vmem = pl.BlockSpec(memory_space=pltpu.VMEM)
    hbm = pl.BlockSpec(memory_space=pl.ANY)
    dma = pltpu.SemaphoreType.DMA
    passed, comb, gain = pl.pallas_call(
        kernel,
        out_shape=(
            jax.ShapeDtypeStruct((TOK, D), BF16),
            jax.ShapeDtypeStruct((TOP, TOK), BF16),
            jax.ShapeDtypeStruct((1, D), F32),
        ),
        in_specs=[hbm] * 8,
        out_specs=(hbm, vmem, vmem),
        scratch_shapes=[
            pltpu.VMEM((TOK, D), BF16),
            pltpu.VMEM((TOK, D), BF16),
            pltpu.VMEM((1, D), F32),
            pltpu.VMEM((TOP, TOK), jnp.int32),
            pltpu.VMEM((TOP, TOK), BF16),
            pltpu.VMEM((16, 16, D), BF16),
            pltpu.VMEM((8, NX, 16, D), BF16),
            pltpu.VMEM((6, HID, D), BF16),
            pltpu.VMEM((32, 16, BACK), BF16),
            pltpu.VMEM((32, 16, BACK), BF16),
            pltpu.VMEM((8, 16, BACK), F32),
            pltpu.VMEM((8, 16, BACK), BF16),
            pltpu.VMEM((TOK, D), BF16),
            pltpu.VMEM((8, D), F32),
            pltpu.VMEM((8, 1, D), F32),
            pltpu.VMEM((8, 1, D), F32),
            dma((5,)), dma((16,)), dma((32,)), dma((16,)), dma((32,)), dma((32,)), dma((8,)),
            dma((3,)), dma((3,)), dma((3,)),
            dma((8,)), dma((8,)), dma((8,)), dma((8,)), dma((2,)),
        ],
        compiler_params=pltpu.CompilerParams(
            collective_id=0, has_side_effects=True, vmem_limit_bytes=60 * 1024 * 1024
        ),
    )(
        layer_input[0], out_grad[0], norm_gain, expert_ids[0].T, combine[0].T,
        w_gate[0], w_up[0], w_down[0],
    )
    return passed[None], comb.T[None], gain


def solution(mesh):
    rows = P("section", "expert", None)
    whole = P("section", None)
    return jax.shard_map(
        per_device,
        mesh=mesh,
        in_specs=(rows, rows, whole, rows, rows, rows, rows, rows),
        out_specs=(rows, rows, whole),
        check_vma=False,
    )
```

```python
import jax
import jax.numpy as jnp
from jax import lax
from jax.experimental import pallas as pl
from jax.experimental.pallas import tpu as pltpu
from jax.sharding import PartitionSpec as P

MESH = pl.DeviceIdType.MESH
NX, NZ = 4, 8
CAP = 8
D = 2048
HALF = D // 2
HID = 192
TOK = 64
TOP = 8
EPS = 1e-06
F32, BF16 = jnp.float32, jnp.bfloat16


def nt(left, right):
    return lax.dot_general(left, right, (((1,), (1,)), ((), ())), preferred_element_type=F32)


def nn(left, right):
    return jnp.dot(left, right, preferred_element_type=F32)


def kernel(
    x_hbm, dy_hbm, g_hbm, ids_hbm, cw_hbm, wg_ref, wu_ref, wd_ref,
    passed_ref, comb_ref, gain_ref,
    x_ref, dy_ref, g_ref, ids_ref, cw_ref,
    next_x, next_dy, next_g, next_ids,
    send, recv, w, ret, got, hold, part, comb_out, comb_in, gain_sum, sum_xc, sum_z,
    in_sem, disp_sem, recv_sem, fwd_sem, ret_sem, got_sem, part_sem, wl_sem, ws_sem, wr_sem,
    push_sem, pushed_sem, cs_sem, cr_sem, xs_sem, xr_sem, zs_sem, zr_sem,
):
    sec = lax.axis_index("section")
    me = lax.axis_index("expert")
    core = lax.rem(me, 2)
    z = lax.rem(me // 2, NZ)
    x = me // (2 * NZ)
    way = 1 - 2 * lax.rem(z, 2)
    mate_z = z + way

    def place(px, pz, pc):
        return (sec, (lax.rem(px + NX, NX) * NZ + lax.rem(pz + 2 * NZ, NZ)) * 2 + pc)

    def entry_z(d):
        return z + way * d if d % 2 == 0 else z - way * d

    sibling = place(x, z, 1 - core)
    mate = place(x, mate_z, core)
    ahead = lax.rem(sec + 7, 8)
    behind = lax.rem(sec + 1, 8)

    fetch = []
    pairs = ((x_hbm, x_ref), (g_hbm, g_ref), (ids_hbm, ids_ref), (cw_hbm, cw_ref), (dy_hbm, dy_ref))
    for n, (src, dst) in enumerate(pairs):
        copy = pltpu.make_async_copy(src, dst, in_sem.at[n])
        copy.start()
        fetch.append(copy)

    barrier = pltpu.get_barrier_semaphore()

    def greet(q, carry):
        chip = lax.rem(x * NZ + z + q, NX * NZ)
        pl.semaphore_signal(barrier, inc=1, device_id=(sec, chip * 2 + core), device_id_type=MESH)
        return carry

    lax.fori_loop(1, NX * NZ, greet, 0)
    for q in range(NX):
        pl.semaphore_signal(
            barrier, inc=1, device_id=place(x + q, z, 1 - core), device_id_type=MESH
        )

    def greet_behind(chip, carry):
        pl.semaphore_signal(
            barrier, inc=1, device_id=(behind, chip * 2 + core), device_id_type=MESH
        )
        return carry

    lax.fori_loop(0, NX * NZ, greet_behind, 0)

    own = []
    for n, ref in enumerate((wg_ref, wu_ref, wd_ref)):
        copy = pltpu.make_async_copy(ref, w.at[2 * n], wl_sem.at[n])
        copy.start()
        own.append(copy)

    for copy in fetch:
        copy.wait()

    rows = x_ref[...].astype(F32)
    rinv = lax.rsqrt(jnp.mean(rows * rows, axis=-1, keepdims=True) + EPS)
    normed = (rows * rinv * g_ref[...]).astype(BF16)
    dy = dy_ref[...]
    ids = ids_ref[...]
    weights = cw_ref[...].astype(F32)

    def expert_of(block):
        d, dx = block // 4, lax.rem(block, 4)
        ez = jnp.where(lax.rem(d, 2) == 0, z + way * d, z - way * d)
        ez = lax.rem(ez + 2 * NZ, NZ)
        return lax.rem(x + dx, NX) * 4 + ez // 2

    before = (
        lax.broadcasted_iota(jnp.int32, (TOK, TOK), 0)
        < lax.broadcasted_iota(jnp.int32, (TOK, TOK), 1)
    ).astype(BF16)

    def picks(ids, weights, slots, per):
        slot = lax.broadcasted_iota(jnp.int32, (slots, TOK), 0)
        expert = expert_of(slot // per)
        named = jnp.zeros((slots, TOK), F32)
        scaled = jnp.zeros((slots, TOK), F32)
        for k in range(TOP):
            hit = ids[k : k + 1, :] == expert
            named = jnp.where(hit, 1.0, named)
            scaled = jnp.where(hit, weights[k : k + 1, :], scaled)
        rank = nn(named.astype(BF16), before)
        mine = rank == lax.rem(slot, CAP).astype(F32)
        return slot, expert, jnp.where(mine, named, 0.0), jnp.where(mine, scaled, 0.0)

    slot, expert, chosen, scaled = picks(ids, weights, 128, CAP)
    token_pick, scaled_pick = chosen.astype(BF16), scaled.astype(BF16)

    def tn(left, right):
        return lax.dot_general(left, right, (((0,), (0,)), ((), ())), preferred_element_type=F32)

    for c in range(4):
        cols = slice(c * 512, (c + 1) * 512)
        part_x = nn(token_pick, normed[:, cols]).reshape(16, CAP, 512)
        part_dy = nn(scaled_pick, dy[:, cols]).reshape(16, CAP, 512)
        send[:, :, cols] = jnp.concatenate([part_x, part_dy], axis=1).astype(BF16)
    recv[0, 0] = send[0]

    pl.semaphore_wait(barrier, 2 * NX * NZ - 1 + NX)

    def dispatch(d, dx):
        return pltpu.make_async_remote_copy(
            src_ref=send.at[d * 4 + dx],
            dst_ref=recv.at[d, dx],
            send_sem=disp_sem.at[d * 4 + dx],
            recv_sem=recv_sem.at[d * 4 + dx],
            device_id=place(x + dx, entry_z(d), core),
            device_id_type=MESH,
        )

    def hand_on(d, dx):
        return pltpu.make_async_remote_copy(
            src_ref=recv.at[d, dx],
            dst_ref=recv.at[d + 4, dx],
            send_sem=fwd_sem.at[d * 4 + dx],
            recv_sem=recv_sem.at[16 + d * 4 + dx],
            device_id=mate,
            device_id_type=MESH,
        )

    def weight_swap(n, ref):
        return pltpu.make_async_remote_copy(
            src_ref=ref,
            dst_ref=w.at[2 * n + 1],
            send_sem=ws_sem.at[n],
            recv_sem=wr_sem.at[n],
            device_id=sibling,
            device_id_type=MESH,
        )

    hand_on(0, 0).start()
    swaps = [weight_swap(n, ref) for n, ref in enumerate((wg_ref, wu_ref, wd_ref))]
    for d in range(4):
        for dx in range(NX):
            if (d, dx) != (0, 0):
                dispatch(d, dx).start()
    for copy in swaps:
        copy.start()

    def push(n, src, dst):
        return pltpu.make_async_remote_copy(
            src_ref=src,
            dst_ref=dst,
            send_sem=push_sem.at[n],
            recv_sem=pushed_sem.at[n],
            device_id=(ahead, me),
            device_id_type=MESH,
        )

    pushes = [
        push(n, src, dst)
        for n, (src, dst) in enumerate(
            ((ids_hbm, next_ids), (g_hbm, next_g), (x_hbm, next_x), (dy_hbm, next_dy))
        )
    ]
    for copy in pushes:
        copy.start()

    def landed(buffer, semaphore):
        pltpu.make_async_copy(buffer, buffer, semaphore).wait()

    def forward(d):
        for dx in range(NX):
            if (d, dx) != (0, 0):
                landed(recv.at[d, dx], recv_sem.at[d * 4 + dx])
                hand_on(d, dx).start()

    def source(g, dx):
        direct = g < 4
        d = jnp.where(direct, g, g - 4)
        return place(x - dx, jnp.where(direct, z - way * d, mate_z + way * d), core)

    def giveback(g, dx):
        return pltpu.make_async_remote_copy(
            src_ref=ret.at[g * 4 + dx],
            dst_ref=got.at[g * 4 + dx],
            send_sem=ret_sem.at[g * 4 + dx],
            recv_sem=got_sem.at[g * 4 + dx],
            device_id=(ahead, source(g, dx)[1]),
            device_id_type=MESH,
        )

    def comb_back(g, dx):
        return pltpu.make_async_remote_copy(
            src_ref=comb_out.at[g],
            dst_ref=comb_in.at[g * 4 + dx],
            send_sem=cs_sem.at[g * 4 + dx],
            recv_sem=cr_sem.at[g * 4 + dx],
            device_id=source(g, dx),
            device_id_type=MESH,
        )

    def halfway(g, dx):
        return pltpu.make_async_remote_copy(
            src_ref=ret.at[g * 4 + dx],
            dst_ref=part.at[(g - 6) * 4 + dx],
            send_sem=ret_sem.at[g * 4 + dx],
            recv_sem=part_sem.at[(g - 6) * 4 + dx],
            device_id=mate,
            device_id_type=MESH,
        )

    def join(d):
        for dx in range(NX):
            n = (d - 2) * 4 + dx
            landed(part.at[n], part_sem.at[n])
            ret[d * 4 + dx] = (hold[n] + part[n].astype(F32)).astype(BF16)
            giveback(d, dx).start()

    forward(0)
    forward(1)
    for copy in own:
        copy.wait()
    for copy in swaps:
        copy.wait()

    gain_sum[...] = jnp.zeros_like(gain_sum)
    on_line = lax.broadcasted_iota(jnp.int32, (32, 128), 0) == lax.broadcasted_iota(
        jnp.int32, (32, 128), 1
    )
    order = (0, 1, 4, 2, 5, 3, 6, 7)

    def group(i, carry):
        g = jnp.int32(order[0])
        for n in range(1, 8):
            g = jnp.where(i == n, order[n], g)

        @pl.when(i == 1)
        def _():
            forward(2)

        @pl.when(i == 2)
        def _():
            forward(3)

        @pl.when(g >= 4)
        def _():
            for dx in range(NX):
                landed(recv.at[g, dx], recv_sem.at[g * 4 + dx])

        block = recv[g].reshape(4 * 16, D)
        gate = nt(block, w[0:2].reshape(2 * HID, D)).reshape(4, 16, 2 * HID)[:, :8]
        upper = nt(block, w[2:4].reshape(2 * HID, D)).reshape(4, 16, 2 * HID)[:, :8]
        down = nt(block, w[4:6].reshape(2 * HID, D)).reshape(4, 16, 2 * HID)[:, 8:]
        sigma = jax.nn.sigmoid(gate)
        active = gate * sigma
        hidden = (active * upper).astype(BF16).astype(F32)
        comb = jnp.sum(hidden * down, axis=-1, keepdims=True)
        gate_part = down * upper * sigma * (1.0 + gate * (1.0 - sigma))
        gate_part = gate_part.reshape(4 * 8, 2 * HID).astype(BF16)
        up_part = (down * active).reshape(4 * 8, 2 * HID).astype(BF16)
        halves = []
        for c in range(2):
            cols = slice(c * HALF, (c + 1) * HALF)
            piece = nn(gate_part, w[0:2, :, cols].reshape(2 * HID, HALF))
            piece += nn(up_part, w[2:4, :, cols].reshape(2 * HID, HALF))
            piece = piece.reshape(4, 8, HALF)
            halves.append(piece)
            held = recv[g, :, :, cols].astype(F32)[:, :8]
            gain_sum[:, cols] += jnp.sum(piece * held, axis=0)
        out = jnp.concatenate(halves, axis=1)
        comb = jnp.where(on_line, comb.reshape(32, 1), 0.0)
        comb_out[g] = jnp.sum(comb, axis=0, keepdims=True)
        kept = (g == 2) | (g == 3)
        half = (g == 6) | (g == 7)

        @pl.when(kept)
        def _():
            for dx in range(NX):
                hold[(g - 2) * 4 + dx] = out[dx]

        @pl.when(jnp.logical_not(kept))
        def _():
            for dx in range(NX):
                ret[g * 4 + dx] = out[dx].astype(BF16)

        @pl.when(half)
        def _():
            for dx in range(NX):
                halfway(g, dx).start()

        @pl.when(jnp.logical_not(kept | half))
        def _():
            for dx in range(NX):
                giveback(g, dx).start()

        @pl.when(g == 0)
        def _():
            comb_in[0] = comb_out[0]

        @pl.when(g > 0)
        def _():
            comb_back(g, 0).start()

        for dx in range(1, NX):
            comb_back(g, dx).start()

        return carry

    lax.fori_loop(0, 8, group, 0)

    sum_xc[x * 2 + core] = jnp.sum(gain_sum[...], axis=0, keepdims=True)

    def share_xc(dx, dc):
        return pltpu.make_async_remote_copy(
            src_ref=sum_xc.at[x * 2 + core],
            dst_ref=sum_xc.at[x * 2 + core],
            send_sem=xs_sem.at[dx * 2 + dc],
            recv_sem=xr_sem.at[dx * 2 + dc],
            device_id=place(x + dx, z, lax.rem(core + dc, 2)),
            device_id_type=MESH,
        )

    others = [(dx, dc) for dx in range(NX) for dc in range(2) if (dx, dc) != (0, 0)]
    for dx, dc in others:
        share_xc(dx, dc).start()

    join(2)
    join(3)

    for dx, dc in others:
        share_xc(dx, dc).wait()
    sum_z[z] = jnp.sum(sum_xc[...], axis=0)

    def share_z(dz):
        return pltpu.make_async_remote_copy(
            src_ref=sum_z.at[z],
            dst_ref=sum_z.at[z],
            send_sem=zs_sem.at[dz],
            recv_sem=zr_sem.at[dz],
            device_id=place(x, z + dz, core),
            device_id_type=MESH,
        )

    for dz in range(1, NZ):
        share_z(dz).start()

    for copy in pushes:
        copy.wait()

    later = next_x[...].astype(F32)
    later_rinv = lax.rsqrt(jnp.mean(later * later, axis=-1, keepdims=True) + EPS)
    row, _, later_pick, _ = picks(next_ids[...], weights, 256, 16)
    first = lax.rem(row, 16) < 8
    low = jnp.where(first, later_pick, 0.0).astype(BF16)
    high = jnp.where(first, 0.0, later_pick).astype(BF16)

    def comb_landed(n, carry):
        landed(comb_in.at[n], cr_sem.at[n])
        return carry

    lax.fori_loop(1, 32, comb_landed, 0)
    found = comb_in[0:16] + comb_in[16:32]
    found = jnp.broadcast_to(found, (16, CAP, 128)).reshape(128, 128)
    spot = lax.rem(lax.broadcasted_iota(jnp.int32, (128, 128), 0), 32)
    spot = spot == lax.broadcasted_iota(jnp.int32, (128, 128), 1)
    found = chosen * jnp.sum(jnp.where(spot, found, 0.0), axis=1, keepdims=True)
    line = lax.broadcasted_iota(jnp.int32, (TOP, TOK), 0)
    comb = jnp.zeros((TOP, TOK), F32)
    for k in range(TOP):
        one = jnp.where(ids[k : k + 1, :] == expert, found, 0.0)
        comb = jnp.where(line == k, jnp.sum(one, axis=0, keepdims=True), comb)
    comb_ref[...] = (comb / weights).astype(BF16)

    for dz in range(1, NZ):
        share_z(dz).wait()
    gain_ref[...] = jnp.sum(sum_z[...], axis=0) / g_ref[...]

    for d in range(4):
        for dx in range(NX):
            if (d, dx) != (0, 0):
                dispatch(d, dx).wait_send()
            hand_on(d, dx).wait_send()

    def sent(n, carry):
        landed(ret.at[n], ret_sem.at[n])
        return carry

    lax.fori_loop(0, 32, sent, 0)

    def comb_sent(n, carry):
        landed(comb_in.at[n], cs_sem.at[n])
        return carry

    lax.fori_loop(1, 32, comb_sent, 0)

    for n in range(24):
        landed(got.at[n], got_sem.at[n])

    total = []
    for side in (low, high):
        sums = tn(side, got[0:16].reshape(256, HALF))
        sums += tn(side[0:128], got[16:24].reshape(128, HALF))
        total.append(sums)
    hats = [next_x[:, c * HALF : (c + 1) * HALF].astype(F32) * later_rinv for c in range(2)]
    scaled_grad = [total[c] * next_g[:, c * HALF : (c + 1) * HALF] for c in range(2)]
    mean = 0.0
    for c in range(2):
        mean += jnp.sum(scaled_grad[c] * hats[c], axis=-1, keepdims=True)
    mean = mean / D
    for c in range(2):
        cols = slice(c * HALF, (c + 1) * HALF)
        grad = next_dy[:, cols].astype(F32) + later_rinv * (scaled_grad[c] - hats[c] * mean)
        passed_ref[:, cols] = jnp.where(sec == 7, 0.0, grad).astype(BF16)


def per_device(layer_input, out_grad, norm_gain, expert_ids, combine, w_gate, w_up, w_down):
    vmem = pl.BlockSpec(memory_space=pltpu.VMEM)
    hbm = pl.BlockSpec(memory_space=pl.ANY)
    dma = pltpu.SemaphoreType.DMA
    passed, comb, gain = pl.pallas_call(
        kernel,
        out_shape=(
            jax.ShapeDtypeStruct((TOK, D), BF16),
            jax.ShapeDtypeStruct((TOP, TOK), BF16),
            jax.ShapeDtypeStruct((1, D), F32),
        ),
        in_specs=[hbm] * 8,
        out_specs=(vmem, vmem, vmem),
        scratch_shapes=[
            pltpu.VMEM((TOK, D), BF16),
            pltpu.VMEM((TOK, D), BF16),
            pltpu.VMEM((1, D), F32),
            pltpu.VMEM((TOP, TOK), jnp.int32),
            pltpu.VMEM((TOP, TOK), BF16),
            pltpu.VMEM((TOK, D), BF16),
            pltpu.VMEM((TOK, D), BF16),
            pltpu.VMEM((1, D), F32),
            pltpu.VMEM((TOP, TOK), jnp.int32),
            pltpu.VMEM((16, 16, D), BF16),
            pltpu.VMEM((8, NX, 16, D), BF16),
            pltpu.VMEM((6, HID, D), BF16),
            pltpu.VMEM((32, 16, HALF), BF16),
            pltpu.VMEM((24, 16, HALF), BF16),
            pltpu.VMEM((8, 16, HALF), F32),
            pltpu.VMEM((8, 16, HALF), BF16),
            pltpu.VMEM((8, 1, 128), F32),
            pltpu.VMEM((32, 1, 128), F32),
            pltpu.VMEM((8, D), F32),
            pltpu.VMEM((8, 1, D), F32),
            pltpu.VMEM((8, 1, D), F32),
            dma((5,)), dma((16,)), dma((32,)), dma((16,)), dma((32,)), dma((24,)), dma((8,)),
            dma((3,)), dma((3,)), dma((3,)),
            dma((4,)), dma((4,)), dma((32,)), dma((32,)), dma((8,)), dma((8,)), dma((8,)), dma((8,)),
        ],
        compiler_params=pltpu.CompilerParams(
            collective_id=0, has_side_effects=True, vmem_limit_bytes=60 * 1024 * 1024
        ),
    )(
        layer_input[0], out_grad[0], norm_gain, expert_ids[0].T, combine[0].T,
        w_gate[0], w_up[0], w_down[0],
    )
    return passed[None], comb.T[None], gain


def solution(mesh):
    rows = P("section", "expert", None)
    whole = P("section", None)
    return jax.shard_map(
        per_device,
        mesh=mesh,
        in_specs=(rows, rows, whole, rows, rows, rows, rows, rows),
        out_specs=(rows, rows, whole),
        check_vma=False,
    )
```

```python
import jax
import jax.numpy as jnp
from jax import lax
from jax.experimental import pallas as pl
from jax.experimental.pallas import tpu as pltpu
from jax.sharding import PartitionSpec as P

MESH = pl.DeviceIdType.MESH
NX, NZ = 4, 8
CAP = 8
D = 2048
HALF = D // 2
HID = 192
TOK = 64
TOP = 8
EPS = 1e-06
F32, BF16 = jnp.float32, jnp.bfloat16


def nt(left, right):
    return lax.dot_general(left, right, (((1,), (1,)), ((), ())), preferred_element_type=F32)


def nn(left, right):
    return jnp.dot(left, right, preferred_element_type=F32)


def kernel(
    x_hbm, dy_hbm, g_hbm, ids_hbm, cw_hbm, wg_ref, wu_ref, wd_ref,
    passed_ref, comb_ref, gain_ref,
    x_ref, dy_ref, g_ref, ids_ref, cw_ref,
    next_x, next_dy, next_g, next_ids,
    send, recv, w, ret, got, hold, part, comb_out, comb_in, gain_sum, sum_xc, sum_z,
    in_sem, disp_sem, recv_sem, fwd_sem, ret_sem, got_sem, part_sem, wl_sem, ws_sem, wr_sem,
    push_sem, pushed_sem, cs_sem, cr_sem, xs_sem, xr_sem, zs_sem, zr_sem,
):
    sec = lax.axis_index("section")
    me = lax.axis_index("expert")
    core = lax.rem(me, 2)
    z = lax.rem(me // 2, NZ)
    x = me // (2 * NZ)
    way = 1 - 2 * lax.rem(z, 2)
    mate_z = z + way

    def place(px, pz, pc):
        return (sec, (lax.rem(px + NX, NX) * NZ + lax.rem(pz + 2 * NZ, NZ)) * 2 + pc)

    def entry_z(d):
        return z + way * d if d % 2 == 0 else z - way * d

    sibling = place(x, z, 1 - core)
    mate = place(x, mate_z, core)
    ahead = lax.rem(sec + 7, 8)
    behind = lax.rem(sec + 1, 8)

    fetch = []
    pairs = ((x_hbm, x_ref), (g_hbm, g_ref), (ids_hbm, ids_ref), (cw_hbm, cw_ref), (dy_hbm, dy_ref))
    for n, (src, dst) in enumerate(pairs):
        copy = pltpu.make_async_copy(src, dst, in_sem.at[n])
        copy.start()
        fetch.append(copy)

    barrier = pltpu.get_barrier_semaphore()

    def greet(q, carry):
        chip = lax.rem(x * NZ + z + q, NX * NZ)
        pl.semaphore_signal(barrier, inc=1, device_id=(sec, chip * 2 + core), device_id_type=MESH)
        return carry

    lax.fori_loop(1, NX * NZ, greet, 0)
    for q in range(NX):
        pl.semaphore_signal(
            barrier, inc=1, device_id=place(x + q, z, 1 - core), device_id_type=MESH
        )

    def greet_behind(chip, carry):
        pl.semaphore_signal(
            barrier, inc=1, device_id=(behind, chip * 2 + core), device_id_type=MESH
        )
        return carry

    lax.fori_loop(0, NX * NZ, greet_behind, 0)

    own = []
    for n, ref in enumerate((wg_ref, wu_ref, wd_ref)):
        copy = pltpu.make_async_copy(ref, w.at[2 * n], wl_sem.at[n])
        copy.start()
        own.append(copy)

    for copy in fetch:
        copy.wait()

    rows = x_ref[...].astype(F32)
    rinv = lax.rsqrt(jnp.mean(rows * rows, axis=-1, keepdims=True) + EPS)
    normed = (rows * rinv * g_ref[...]).astype(BF16)
    dy = dy_ref[...]
    ids = ids_ref[...]
    weights = cw_ref[...].astype(F32)

    def expert_of(block):
        d, dx = block // 4, lax.rem(block, 4)
        ez = jnp.where(lax.rem(d, 2) == 0, z + way * d, z - way * d)
        ez = lax.rem(ez + 2 * NZ, NZ)
        return lax.rem(x + dx, NX) * 4 + ez // 2

    before = (
        lax.broadcasted_iota(jnp.int32, (TOK, TOK), 0)
        < lax.broadcasted_iota(jnp.int32, (TOK, TOK), 1)
    ).astype(BF16)

    def picks(ids, weights, slots, per):
        slot = lax.broadcasted_iota(jnp.int32, (slots, TOK), 0)
        expert = expert_of(slot // per)
        named = jnp.zeros((slots, TOK), F32)
        scaled = jnp.zeros((slots, TOK), F32)
        for k in range(TOP):
            hit = ids[k : k + 1, :] == expert
            named = jnp.where(hit, 1.0, named)
            scaled = jnp.where(hit, weights[k : k + 1, :], scaled)
        rank = nn(named.astype(BF16), before)
        mine = rank == lax.rem(slot, CAP).astype(F32)
        return slot, expert, jnp.where(mine, named, 0.0), jnp.where(mine, scaled, 0.0)

    slot, expert, chosen, scaled = picks(ids, weights, 128, CAP)
    token_pick, scaled_pick = chosen.astype(BF16), scaled.astype(BF16)

    def tn(left, right):
        return lax.dot_general(left, right, (((0,), (0,)), ((), ())), preferred_element_type=F32)

    for c in range(4):
        cols = slice(c * 512, (c + 1) * 512)
        part_x = nn(token_pick, normed[:, cols]).reshape(16, CAP, 512)
        part_dy = nn(scaled_pick, dy[:, cols]).reshape(16, CAP, 512)
        send[:, :, cols] = jnp.concatenate([part_x, part_dy], axis=1).astype(BF16)
    recv[0, 0] = send[0]

    pl.semaphore_wait(barrier, 2 * NX * NZ - 1 + NX)

    def dispatch(d, dx):
        return pltpu.make_async_remote_copy(
            src_ref=send.at[d * 4 + dx],
            dst_ref=recv.at[d, dx],
            send_sem=disp_sem.at[d * 4 + dx],
            recv_sem=recv_sem.at[d * 4 + dx],
            device_id=place(x + dx, entry_z(d), core),
            device_id_type=MESH,
        )

    def hand_on(d, dx):
        return pltpu.make_async_remote_copy(
            src_ref=recv.at[d, dx],
            dst_ref=recv.at[d + 4, dx],
            send_sem=fwd_sem.at[d * 4 + dx],
            recv_sem=recv_sem.at[16 + d * 4 + dx],
            device_id=mate,
            device_id_type=MESH,
        )

    def weight_swap(n, ref):
        return pltpu.make_async_remote_copy(
            src_ref=ref,
            dst_ref=w.at[2 * n + 1],
            send_sem=ws_sem.at[n],
            recv_sem=wr_sem.at[n],
            device_id=sibling,
            device_id_type=MESH,
        )

    hand_on(0, 0).start()
    swaps = [weight_swap(n, ref) for n, ref in enumerate((wg_ref, wu_ref, wd_ref))]
    for d in (0, 1, 2, 3):
        for dx in range(NX):
            if (d, dx) != (0, 0):
                dispatch(d, dx).start()
    for copy in swaps:
        copy.start()

    def push(n, src, dst):
        return pltpu.make_async_remote_copy(
            src_ref=src,
            dst_ref=dst,
            send_sem=push_sem.at[n],
            recv_sem=pushed_sem.at[n],
            device_id=(ahead, me),
            device_id_type=MESH,
        )

    pushes = [
        push(n, src, dst)
        for n, (src, dst) in enumerate(
            ((ids_hbm, next_ids), (g_hbm, next_g), (x_hbm, next_x), (dy_hbm, next_dy))
        )
    ]
    for copy in pushes:
        copy.start()

    def landed(buffer, semaphore):
        pltpu.make_async_copy(buffer, buffer, semaphore).wait()

    def forward(d):
        for dx in range(NX):
            if (d, dx) != (0, 0):
                landed(recv.at[d, dx], recv_sem.at[d * 4 + dx])
                hand_on(d, dx).start()

    def source(g, dx):
        direct = g < 4
        d = jnp.where(direct, g, g - 4)
        return place(x - dx, jnp.where(direct, z - way * d, mate_z + way * d), core)

    def giveback(g, dx):
        return pltpu.make_async_remote_copy(
            src_ref=ret.at[g * 4 + dx],
            dst_ref=got.at[g * 4 + dx],
            send_sem=ret_sem.at[g * 4 + dx],
            recv_sem=got_sem.at[g * 4 + dx],
            device_id=(ahead, source(g, dx)[1]),
            device_id_type=MESH,
        )

    def comb_back(g, dx):
        return pltpu.make_async_remote_copy(
            src_ref=comb_out.at[g],
            dst_ref=comb_in.at[g * 4 + dx],
            send_sem=cs_sem.at[g * 4 + dx],
            recv_sem=cr_sem.at[g * 4 + dx],
            device_id=source(g, dx),
            device_id_type=MESH,
        )

    def halfway(g, dx):
        return pltpu.make_async_remote_copy(
            src_ref=ret.at[g * 4 + dx],
            dst_ref=part.at[(g - 6) * 4 + dx],
            send_sem=ret_sem.at[g * 4 + dx],
            recv_sem=part_sem.at[(g - 6) * 4 + dx],
            device_id=mate,
            device_id_type=MESH,
        )

    def join(d):
        for dx in range(NX):
            n = (d - 2) * 4 + dx
            landed(part.at[n], part_sem.at[n])
            ret[d * 4 + dx] = (hold[n] + part[n].astype(F32)).astype(BF16)
            giveback(d, dx).start()

    forward(0)
    forward(1)
    for copy in own:
        copy.wait()
    for copy in swaps:
        copy.wait()

    gain_sum[...] = jnp.zeros_like(gain_sum)
    on_line = lax.broadcasted_iota(jnp.int32, (32, 128), 0) == lax.broadcasted_iota(
        jnp.int32, (32, 128), 1
    )
    order = (0, 4, 1, 5, 2, 3, 6, 7)

    def group(i, carry):
        g = jnp.int32(order[0])
        for n in range(1, 8):
            g = jnp.where(i == n, order[n], g)

        @pl.when(i == 1)
        def _():
            forward(2)

        @pl.when(i == 3)
        def _():
            forward(3)

        @pl.when(g >= 4)
        def _():
            for dx in range(NX):
                landed(recv.at[g, dx], recv_sem.at[g * 4 + dx])

        block = recv[g].reshape(4 * 16, D)
        gate = nt(block, w[0:2].reshape(2 * HID, D)).reshape(4, 16, 2 * HID)[:, :8]
        upper = nt(block, w[2:4].reshape(2 * HID, D)).reshape(4, 16, 2 * HID)[:, :8]
        down = nt(block, w[4:6].reshape(2 * HID, D)).reshape(4, 16, 2 * HID)[:, 8:]
        sigma = jax.nn.sigmoid(gate)
        active = gate * sigma
        hidden = (active * upper).astype(BF16).astype(F32)
        comb = jnp.sum(hidden * down, axis=-1, keepdims=True)
        gate_part = down * upper * sigma * (1.0 + gate * (1.0 - sigma))
        gate_part = gate_part.reshape(4 * 8, 2 * HID).astype(BF16)
        up_part = (down * active).reshape(4 * 8, 2 * HID).astype(BF16)
        halves = []
        for c in range(2):
            cols = slice(c * HALF, (c + 1) * HALF)
            piece = nn(gate_part, w[0:2, :, cols].reshape(2 * HID, HALF))
            piece += nn(up_part, w[2:4, :, cols].reshape(2 * HID, HALF))
            piece = piece.reshape(4, 8, HALF)
            halves.append(piece)
            held = recv[g, :, :, cols].astype(F32)[:, :8]
            gain_sum[:, cols] += jnp.sum(piece * held, axis=0)
        out = jnp.concatenate(halves, axis=1)
        comb = jnp.where(on_line, comb.reshape(32, 1), 0.0)
        comb_out[g] = jnp.sum(comb, axis=0, keepdims=True)
        kept = (g == 2) | (g == 3)
        half = (g == 6) | (g == 7)

        @pl.when(kept)
        def _():
            for dx in range(NX):
                hold[(g - 2) * 4 + dx] = out[dx]

        @pl.when(jnp.logical_not(kept))
        def _():
            for dx in range(NX):
                ret[g * 4 + dx] = out[dx].astype(BF16)

        @pl.when(half)
        def _():
            for dx in range(NX):
                halfway(g, dx).start()

        @pl.when(jnp.logical_not(kept | half))
        def _():
            for dx in range(NX):
                giveback(g, dx).start()

        @pl.when(g == 0)
        def _():
            comb_in[0] = comb_out[0]

        @pl.when(g > 0)
        def _():
            comb_back(g, 0).start()

        for dx in range(1, NX):
            comb_back(g, dx).start()

        return carry

    lax.fori_loop(0, 8, group, 0)

    sum_xc[x * 2 + core] = jnp.sum(gain_sum[...], axis=0, keepdims=True)

    def share_xc(dx, dc):
        return pltpu.make_async_remote_copy(
            src_ref=sum_xc.at[x * 2 + core],
            dst_ref=sum_xc.at[x * 2 + core],
            send_sem=xs_sem.at[dx * 2 + dc],
            recv_sem=xr_sem.at[dx * 2 + dc],
            device_id=place(x + dx, z, lax.rem(core + dc, 2)),
            device_id_type=MESH,
        )

    others = [(dx, dc) for dx in range(NX) for dc in range(2) if (dx, dc) != (0, 0)]
    for dx, dc in others:
        share_xc(dx, dc).start()

    join(2)
    join(3)

    for dx, dc in others:
        share_xc(dx, dc).wait()
    sum_z[z] = jnp.sum(sum_xc[...], axis=0)

    def share_z(dz):
        return pltpu.make_async_remote_copy(
            src_ref=sum_z.at[z],
            dst_ref=sum_z.at[z],
            send_sem=zs_sem.at[dz],
            recv_sem=zr_sem.at[dz],
            device_id=place(x, z + dz, core),
            device_id_type=MESH,
        )

    for dz in range(1, NZ):
        share_z(dz).start()

    for copy in pushes:
        copy.wait()

    later = next_x[...].astype(F32)
    later_rinv = lax.rsqrt(jnp.mean(later * later, axis=-1, keepdims=True) + EPS)
    row, _, later_pick, _ = picks(next_ids[...], weights, 256, 16)
    first = lax.rem(row, 16) < 8
    low = jnp.where(first, later_pick, 0.0).astype(BF16)
    high = jnp.where(first, 0.0, later_pick).astype(BF16)

    def comb_landed(n, carry):
        landed(comb_in.at[n], cr_sem.at[n])
        return carry

    lax.fori_loop(1, 32, comb_landed, 0)
    found = comb_in[0:16] + comb_in[16:32]
    found = jnp.broadcast_to(found, (16, CAP, 128)).reshape(128, 128)
    spot = lax.rem(lax.broadcasted_iota(jnp.int32, (128, 128), 0), 32)
    spot = spot == lax.broadcasted_iota(jnp.int32, (128, 128), 1)
    found = chosen * jnp.sum(jnp.where(spot, found, 0.0), axis=1, keepdims=True)
    line = lax.broadcasted_iota(jnp.int32, (TOP, TOK), 0)
    comb = jnp.zeros((TOP, TOK), F32)
    for k in range(TOP):
        one = jnp.where(ids[k : k + 1, :] == expert, found, 0.0)
        comb = jnp.where(line == k, jnp.sum(one, axis=0, keepdims=True), comb)
    comb_ref[...] = (comb / weights).astype(BF16)

    for dz in range(1, NZ):
        share_z(dz).wait()
    gain_ref[...] = jnp.sum(sum_z[...], axis=0) / g_ref[...]

    for d in range(4):
        for dx in range(NX):
            if (d, dx) != (0, 0):
                dispatch(d, dx).wait_send()
            hand_on(d, dx).wait_send()

    def sent(n, carry):
        landed(ret.at[n], ret_sem.at[n])
        return carry

    lax.fori_loop(0, 32, sent, 0)

    def comb_sent(n, carry):
        landed(comb_in.at[n], cs_sem.at[n])
        return carry

    lax.fori_loop(1, 32, comb_sent, 0)

    for n in range(24):
        landed(got.at[n], got_sem.at[n])

    total = []
    for side in (low, high):
        sums = tn(side, got[0:16].reshape(256, HALF))
        sums += tn(side[0:128], got[16:24].reshape(128, HALF))
        total.append(sums)
    hats = [next_x[:, c * HALF : (c + 1) * HALF].astype(F32) * later_rinv for c in range(2)]
    scaled_grad = [total[c] * next_g[:, c * HALF : (c + 1) * HALF] for c in range(2)]
    mean = 0.0
    for c in range(2):
        mean += jnp.sum(scaled_grad[c] * hats[c], axis=-1, keepdims=True)
    mean = mean / D
    for c in range(2):
        cols = slice(c * HALF, (c + 1) * HALF)
        grad = next_dy[:, cols].astype(F32) + later_rinv * (scaled_grad[c] - hats[c] * mean)
        passed_ref[:, cols] = jnp.where(sec == 7, 0.0, grad).astype(BF16)


def per_device(layer_input, out_grad, norm_gain, expert_ids, combine, w_gate, w_up, w_down):
    vmem = pl.BlockSpec(memory_space=pltpu.VMEM)
    hbm = pl.BlockSpec(memory_space=pl.ANY)
    dma = pltpu.SemaphoreType.DMA
    passed, comb, gain = pl.pallas_call(
        kernel,
        out_shape=(
            jax.ShapeDtypeStruct((TOK, D), BF16),
            jax.ShapeDtypeStruct((TOP, TOK), BF16),
            jax.ShapeDtypeStruct((1, D), F32),
        ),
        in_specs=[hbm] * 8,
        out_specs=(vmem, vmem, vmem),
        scratch_shapes=[
            pltpu.VMEM((TOK, D), BF16),
            pltpu.VMEM((TOK, D), BF16),
            pltpu.VMEM((1, D), F32),
            pltpu.VMEM((TOP, TOK), jnp.int32),
            pltpu.VMEM((TOP, TOK), BF16),
            pltpu.VMEM((TOK, D), BF16),
            pltpu.VMEM((TOK, D), BF16),
            pltpu.VMEM((1, D), F32),
            pltpu.VMEM((TOP, TOK), jnp.int32),
            pltpu.VMEM((16, 16, D), BF16),
            pltpu.VMEM((8, NX, 16, D), BF16),
            pltpu.VMEM((6, HID, D), BF16),
            pltpu.VMEM((32, 16, HALF), BF16),
            pltpu.VMEM((24, 16, HALF), BF16),
            pltpu.VMEM((8, 16, HALF), F32),
            pltpu.VMEM((8, 16, HALF), BF16),
            pltpu.VMEM((8, 1, 128), F32),
            pltpu.VMEM((32, 1, 128), F32),
            pltpu.VMEM((8, D), F32),
            pltpu.VMEM((8, 1, D), F32),
            pltpu.VMEM((8, 1, D), F32),
            dma((5,)), dma((16,)), dma((32,)), dma((16,)), dma((32,)), dma((24,)), dma((8,)),
            dma((3,)), dma((3,)), dma((3,)),
            dma((4,)), dma((4,)), dma((32,)), dma((32,)), dma((8,)), dma((8,)), dma((8,)), dma((8,)),
        ],
        compiler_params=pltpu.CompilerParams(
            collective_id=0, has_side_effects=True, vmem_limit_bytes=60 * 1024 * 1024
        ),
    )(
        layer_input[0], out_grad[0], norm_gain, expert_ids[0].T, combine[0].T,
        w_gate[0], w_up[0], w_down[0],
    )
    return passed[None], comb.T[None], gain


def solution(mesh):
    rows = P("section", "expert", None)
    whole = P("section", None)
    return jax.shard_map(
        per_device,
        mesh=mesh,
        in_specs=(rows, rows, whole, rows, rows, rows, rows, rows),
        out_specs=(rows, rows, whole),
        check_vma=False,
    )
```
